512 devices in a mesh: dp: 16 (over y, core), ctx: 32 (over z, x).
Axes of the slice: x: 4, y: 8, z: 8, core: 2. Of those that a mesh axis runs over, the one named last changes fastest.
Arguments:
- queries: bfloat16 [16, 4096, 1536], P('dp', 'ctx'), may hold values from -6 to 6
- keys: bfloat16 [16, 4096, 1536], P('dp', 'ctx'), may hold values from -6 to 6
- values: bfloat16 [16, 4096, 1536], P('dp', 'ctx'), may hold values from -6 to 6
- out_grad: bfloat16 [16, 4096, 1536], P('dp', 'ctx'), may hold values from -54 to 54
- norm_gains: float32 [2, 128], replicated, may hold values from 0.5 to 8
- tile_image: int32 [16, 16], P('dp'), may hold values from 0 to 11, never falling along the last dimension, each value on 1 to 2 neighbouring positions
Outputs:
- query_grad: bfloat16 [16, 4096, 1536], P('dp', 'ctx')
- key_grad: bfloat16 [16, 4096, 1536], P('dp', 'ctx')
- value_grad: bfloat16 [16, 4096, 1536], P('dp', 'ctx')
- gain_grad: float32 [2, 128], replicated
The draws below stay inside these ranges and needn't reach their ends.
Inputs may be any that keep to these rules, and one draw needn't show every extreme that they name: `tile_image`: each tile is 256 consecutive positions of the replica's packed sequence.
All inputs are finite; a program needn't handle non-finite values.
Results may differ from the reference program's by a relative error of at most 0.0075.
The reference program's roundings to bfloat16 on the way (of `score_grad`) count: a program that leaves them out, or rounds other values in their place, can miss the bound.
Values may be sent and summed in bfloat16 or wider, within the bound.
No kernel may reach another device: no remote copies, remote signals or barrier semaphores. Data moves between devices by JAX's collectives and lax.ppermute only.
A program may use at most 64 MiB of HBM per device.

```python
import math
import jax
import jax.numpy as jnp
import numpy as np
from jax import lax

HEADS = 12
HEAD_DIM = 128
TILE = 256
OWN_TILES = 2
TOK_DEV = 128
REPLICAS = 16
SEQ = 4096
WIDTH = 1536
TILES = 16
IMAGES = 12


def pair_base(key):
    shard_count = SEQ // TOK_DEV
    return jax.random.normal(key, (REPLICAS, shard_count // 2, TOK_DEV, HEADS, HEAD_DIM), jnp.float32)


def draw_keys(key, part):
    shared_base = pair_base(key)
    key = jax.random.fold_in(key, 11)
    paired_rows = jax.random.normal(key, shared_base.shape[:2] + (2,) + shared_base.shape[2:], jnp.float32)
    return jnp.clip(paired_rows.reshape(REPLICAS, SEQ, HEADS * HEAD_DIM), -6.0, 6.0).astype(jnp.bfloat16)


def draw_queries(key, part):
    shared_base = pair_base(key)
    key = jax.random.fold_in(key, 12)
    key_one = jax.random.fold_in(key, 0)
    drawn_rows = jax.random.normal(key_one, shared_base.shape[:2] + (2,) + shared_base.shape[2:], jnp.float32)
    return jnp.clip(drawn_rows.reshape(REPLICAS, SEQ, HEADS * HEAD_DIM), -6.0, 6.0).astype(jnp.bfloat16)


def draw_out_grad(key, part):
    key = jax.random.fold_in(key, 13)
    noise_rows = jnp.clip(jax.random.normal(key, (REPLICAS, SEQ, HEADS * HEAD_DIM), jnp.float32), -6.0, 6.0)
    rank_along = (jnp.arange(REPLICAS)[:, None] * SEQ + jnp.arange(SEQ)[None, :]).astype(jnp.float32) / (REPLICAS * SEQ - 1)
    growth = 3.0
    return (noise_rows * growth ** rank_along[..., None]).astype(jnp.bfloat16)


def draw_norm_gains(key, part):
    key = jax.random.fold_in(key, 14)
    return jnp.exp(jax.random.uniform(key, (2, HEAD_DIM), jnp.float32, jnp.log(0.5), jnp.log(2.0)))


def levels(own_key, extent, cuts, smallest, top_value):
    level = 1.0
    for position, blocks in cuts:
        steps = jax.random.uniform(jax.random.fold_in(jax.random.fold_in(own_key, 6), position), (blocks,), jnp.float32, smallest / len(cuts), top_value / len(cuts))
        level = level * jnp.repeat(jnp.exp(steps), extent[position] // blocks).reshape((-1,) + (1,) * (len(extent) - 1 - position))
    return level


def split_up(number_of, total, most, slope):
    portions = [(1 << 20) // math.isqrt(rank ** slope) + 1 for rank in range(2, number_of + 1)]
    spare, counts = total - most - (number_of - 1), [1] * (number_of - 1)
    while spare > 0:
        candidates = [i for i in range(number_of - 1) if counts[i] < most]
        whole, remaining = sum([portions[i] for i in candidates]), spare
        for i in candidates:
            addition = min(most - counts[i], max(1, remaining * portions[i] // whole), spare)
            counts[i] = counts[i] + addition
            spare = spare - addition
    return np.array([most] + counts)


def uneven_parts(stream_key, count, total, reach, slope):
    if count == 2:
        one = jax.random.randint(stream_key, (), max(1, total - reach), min(reach, total - 1) + 1)
        return jnp.stack([one, total - one])
    sizes = jnp.asarray(split_up(count, total, reach, slope), jnp.int32)
    twos = (count - 1) // 2
    giver, receiver = sizes[1:1 + 2 * twos:2], sizes[2:2 + 2 * twos:2]
    room = jnp.minimum(giver - 1, reach - receiver)
    passed = jax.random.randint(jax.random.fold_in(stream_key, 1), (twos,), 0, 1 << 20) % (room + 1)
    sizes = sizes.at[1:1 + 2 * twos:2].set(giver - passed).at[2:2 + 2 * twos:2].set(receiver + passed)
    return sizes[jax.random.permutation(jax.random.fold_in(stream_key, 2), count)]


def gaussian(rng, extent, scale, most, pieces=(), kind=jnp.bfloat16):
    loudness = levels(rng, extent, pieces, -0.22, 0.18) if pieces else 1.0
    drawn = jax.random.normal(rng, extent, jnp.float32) * scale * loudness
    return jnp.minimum(jnp.maximum(drawn, -most), most).astype(kind)


def setup_inputs(seed: int = 0) -> dict:
    arg_keys = jax.random.split(jax.random.key(seed), 7)
    return {
        "queries": draw_queries(jax.random.fold_in(arg_keys[6], 71), 0),
        "keys": draw_keys(jax.random.fold_in(arg_keys[6], 71), 0),
        "values": gaussian(arg_keys[2], (REPLICAS, SEQ, WIDTH), 1.0, 6.0, ((0, 16), (1, 32))),
        "out_grad": draw_out_grad(jax.random.fold_in(arg_keys[6], 71), 0),
        "norm_gains": draw_norm_gains(jax.random.fold_in(arg_keys[6], 71), 0),
        "tile_image": jax.vmap(lambda own: jnp.searchsorted(jnp.cumsum(uneven_parts(own, IMAGES, TILES, OWN_TILES, 0)), jnp.arange(TILES), side="right"))(jax.random.split(arg_keys[5], REPLICAS)).reshape((REPLICAS, TILES)).astype(jnp.int32),
    }


epsilon = 1e-06

def settle(source):
    return lax.optimization_barrier(source.astype(jnp.bfloat16))

def normalize(token_rows, gain):
    row_count = token_rows.shape[0]
    raw_values = token_rows.astype(jnp.float32).reshape(row_count, HEADS, HEAD_DIM)
    inverse = lax.rsqrt(lax.optimization_barrier(jnp.mean(raw_values * raw_values, axis=-1, keepdims=True)) + epsilon)
    unit_rows = raw_values * inverse
    return (unit_rows, inverse, settle(unit_rows * gain).reshape(row_count, HEADS * HEAD_DIM))

def norm_back(grad_norm, unit_rows, inverse, gain):
    grad_values = grad_norm.astype(jnp.float32).reshape(unit_rows.shape)
    direct = grad_values * gain
    inner_term = lax.optimization_barrier(jnp.mean(direct * unit_rows, axis=-1, keepdims=True))
    result = inverse * (direct - unit_rows * inner_term)
    return (result.reshape(unit_rows.shape[0], HEADS * HEAD_DIM).astype(jnp.bfloat16), lax.optimization_barrier(jnp.sum(grad_values * unit_rows, axis=(0, 1))))

def sequence_grads(query_norm, key_norm, value_rows, grad_rows, images):
    tile_count = SEQ // TILE
    score_scale = 1.0 / math.sqrt(HEAD_DIM)

    def tiled(source):
        blocks = source.reshape(tile_count, TILE, HEADS, HEAD_DIM)
        return jnp.pad(blocks, ((1, 1), (0, 0), (0, 0), (0, 0)))
    query_pad = tiled(query_norm)
    key_pad = tiled(key_norm)
    value_pad = tiled(value_rows)
    grad_pad = tiled(grad_rows)
    image_pad = jnp.pad(images, 1, constant_values=-1)

    def window_rows(padded, tile_index):
        return lax.dynamic_slice_in_dim(padded, tile_index, 3, 0).reshape(3 * TILE, HEADS, HEAD_DIM).astype(jnp.float32)

    def center(padded, tile_index):
        return lax.dynamic_index_in_dim(padded, tile_index + 1, 0, keepdims=False)

    def same_mask(tile_index):
        window = lax.dynamic_slice_in_dim(image_pad, tile_index, 3, 0)
        return jnp.repeat(window == center(image_pad, tile_index), TILE)

    def query_side(tile_index):
        query_rows = center(query_pad, tile_index).astype(jnp.float32)
        keys_near = window_rows(key_pad, tile_index)
        values_near = window_rows(value_pad, tile_index)
        grad_tile = center(grad_pad, tile_index).astype(jnp.float32)
        matching = same_mask(tile_index)
        scores = jnp.einsum('qhd,khd->hqk', query_rows, keys_near) * score_scale
        scores = jnp.where(matching[None, None, :], scores, -jnp.inf)
        row_top = lax.optimization_barrier(jnp.max(scores, axis=-1, keepdims=True))
        log_total = row_top + jnp.log(lax.optimization_barrier(jnp.sum(jnp.exp(scores - row_top), axis=-1, keepdims=True)))
        weights = jnp.exp(scores - log_total)
        weight_grad = jnp.einsum('qhd,khd->hqk', grad_tile, values_near)
        row_inner = lax.optimization_barrier(jnp.sum(weights * weight_grad, axis=-1, keepdims=True))
        score_grad = settle(weights * (weight_grad - row_inner)).astype(jnp.float32)
        query_grad = jnp.einsum('hqk,khd->qhd', score_grad, keys_near) * score_scale
        return (settle(query_grad), log_total[..., 0], row_inner[..., 0])
    tile_range = jnp.arange(tile_count, dtype=jnp.int32)
    query_grads, log_totals, row_inners = lax.map(query_side, tile_range)

    def stat_pad(statistic):
        return jnp.pad(jnp.transpose(statistic, (1, 0, 2)), ((0, 0), (1, 1), (0, 0)))
    total_pad = stat_pad(log_totals)
    inner_pad = stat_pad(row_inners)

    def key_side(tile_index):
        keys_here = center(key_pad, tile_index).astype(jnp.float32)
        values_here = center(value_pad, tile_index).astype(jnp.float32)
        queries_near = window_rows(query_pad, tile_index)
        grads_near = window_rows(grad_pad, tile_index)
        totals_near = lax.dynamic_slice_in_dim(total_pad, tile_index, 3, 1).reshape(HEADS, 3 * TILE)
        inners_near = lax.dynamic_slice_in_dim(inner_pad, tile_index, 3, 1).reshape(HEADS, 3 * TILE)
        matching = same_mask(tile_index)
        scores = jnp.einsum('qhd,khd->hqk', queries_near, keys_here) * score_scale
        weights = jnp.where(matching[None, :, None], jnp.exp(scores - totals_near[..., None]), 0.0)
        weight_grad = jnp.einsum('qhd,khd->hqk', grads_near, values_here)
        score_grad = settle(weights * (weight_grad - inners_near[..., None])).astype(jnp.float32)
        value_grad = jnp.einsum('hqk,qhd->khd', settle(weights).astype(jnp.float32), grads_near)
        key_grad = jnp.einsum('hqk,qhd->khd', score_grad, queries_near) * score_scale
        return (settle(key_grad), settle(value_grad))
    key_grads, value_grads = lax.map(key_side, tile_range)
    return (query_grads.reshape(SEQ, HEADS * HEAD_DIM), key_grads.reshape(SEQ, HEADS * HEAD_DIM), value_grads.reshape(SEQ, HEADS * HEAD_DIM))

def reference(queries, keys, values, out_grad, norm_gains, tile_image):
    shards = SEQ // TOK_DEV
    positions = (jnp.arange(TOK_DEV, dtype=jnp.int32)[None, :] * shards + jnp.arange(shards, dtype=jnp.int32)[:, None]).reshape(SEQ)

    def ordered(source):
        return jnp.zeros_like(source).at[positions].set(source)

    def replica(inputs):
        query_rows, key_rows, value_rows, grad_rows, images = inputs
        query_unit, query_inverse, query_norm = normalize(query_rows, norm_gains[0])
        key_unit, key_inverse, key_norm = normalize(key_rows, norm_gains[1])
        in_order = sequence_grads(ordered(query_norm), ordered(key_norm), ordered(value_rows), ordered(grad_rows), images)
        query_norm_grad = in_order[0][positions]
        key_norm_grad = in_order[1][positions]
        value_grad = in_order[2][positions]
        query_grad, query_term = norm_back(query_norm_grad, query_unit, query_inverse, norm_gains[0])
        key_grad, key_term = norm_back(key_norm_grad, key_unit, key_inverse, norm_gains[1])
        return (query_grad, key_grad, value_grad, jnp.stack([query_term, key_term]))
    query_grad, key_grad, value_grad, gain_terms = lax.map(replica, (queries, keys, values, out_grad, tile_image))
    return (query_grad, key_grad, value_grad, lax.optimization_barrier(jnp.sum(gain_terms, axis=0)))
```

```python
import math

import jax
import jax.numpy as jnp
from jax import lax
from jax.experimental import pallas as pl
from jax.experimental.pallas import tpu as pltpu
from jax.sharding import PartitionSpec as P

epsilon = 1e-06

GROUPS = 4
SLOTS = 2
PIECE_ROWS = 8
HEAD_DIM = 128


def packed_places(image_ref, tile_count):
    images = [image_ref[0, t] for t in range(tile_count)]
    one = jnp.int32(1)
    zero = jnp.int32(0)
    joined = [zero] + [
        jnp.where(images[t] == images[t - 1], one, zero) for t in range(1, tile_count)
    ]
    long_count = sum(joined[1:], zero)
    long_next = zero
    short_next = long_count * 2
    places = []
    for t in range(tile_count):
        ahead = joined[t + 1] if t + 1 < tile_count else zero
        in_long = joined[t] + ahead
        places.append(jnp.where(in_long > 0, long_next, short_next))
        long_next = long_next + in_long
        short_next = short_next + (1 - in_long)
    return places, long_count


def pack_kernel(image_ref, *refs):
    sources, out_ref = refs[:-1], refs[-1]
    tile_count = sources[0].shape[0]
    heads = sources[0].shape[2] // HEAD_DIM
    per_group = heads // GROUPS
    places, _ = packed_places(image_ref, tile_count)
    for t in range(tile_count):
        pair = places[t] // SLOTS
        slot = places[t] % SLOTS
        for a, source in enumerate(sources):
            for c in range(heads):
                out_ref[
                    pair * GROUPS + c // per_group,
                    (a * per_group + c % per_group) * SLOTS + slot,
                ] = source[t, :, c * HEAD_DIM : (c + 1) * HEAD_DIM]


def unpack_kernel(image_ref, blocks_ref, *outs):
    tile_count = outs[0].shape[0]
    heads = outs[0].shape[2] // HEAD_DIM
    per_group = heads // GROUPS
    places, _ = packed_places(image_ref, tile_count)
    for t in range(tile_count):
        pair = places[t] // SLOTS
        slot = places[t] % SLOTS
        for a, out in enumerate(outs):
            for c in range(heads):
                out[t, :, c * HEAD_DIM : (c + 1) * HEAD_DIM] = blocks_ref[
                    pair * GROUPS + c // per_group,
                    (a * per_group + c % per_group) * SLOTS + slot,
                ]


def work_kernel(per_group, place_ref, image_ref, gains_ref, blocks_ref, out_ref):
    shards = blocks_ref.shape[0]
    tile_count = image_ref.shape[1]
    rows = shards * SLOTS * PIECE_ROWS
    scale = 1.0 / math.sqrt(HEAD_DIM)
    f32, bf16 = jnp.float32, jnp.bfloat16
    _, long_count = packed_places(image_ref, tile_count)
    is_long = place_ref[0] // GROUPS < long_count

    period = SLOTS * PIECE_ROWS
    key_slot = lax.broadcasted_iota(jnp.int32, (period, rows), 0) // PIECE_ROWS % SLOTS
    query_slot = lax.broadcasted_iota(jnp.int32, (period, rows), 1) // PIECE_ROWS % SLOTS
    apart = jnp.where(is_long, 0.0, -1e30).astype(f32)
    bias = jnp.where(key_slot == query_slot, jnp.zeros((), f32), apart)

    def load(a, h):
        first = (a * per_group + h) * SLOTS
        return blocks_ref[:, first : first + SLOTS].astype(f32).reshape(rows, HEAD_DIM)

    def store(a, h, value):
        first = (a * per_group + h) * SLOTS
        out_ref[:, first : first + SLOTS] = value.reshape(
            shards, SLOTS, PIECE_ROWS, HEAD_DIM
        ).astype(bf16)

    def normalize(raw, gain):
        inverse = lax.rsqrt(jnp.mean(raw * raw, axis=-1, keepdims=True) + epsilon)
        unit = raw * inverse
        return unit, inverse, (unit * gain).astype(bf16)

    def norm_back(grad_norm, unit, inverse, gain):
        grad = grad_norm.astype(bf16).astype(f32)
        direct = grad * gain
        inner = jnp.mean(direct * unit, axis=-1, keepdims=True)
        return inverse * (direct - unit * inner), jnp.sum(grad * unit, axis=0, keepdims=True)

    def dot(a, b, dims):
        return lax.dot_general(a, b, (dims, ((), ())), preferred_element_type=f32)

    query_gain = gains_ref[0:1, :]
    key_gain = gains_ref[1:2, :]
    query_term = jnp.zeros((1, HEAD_DIM), f32)
    key_term = jnp.zeros((1, HEAD_DIM), f32)
    for h in range(per_group):
        query_unit, query_inverse, query_norm = normalize(load(0, h), query_gain)
        key_unit, key_inverse, key_norm = normalize(load(1, h), key_gain)
        value = load(2, h).astype(bf16)
        grad = load(3, h).astype(bf16)
        scores = dot(key_norm, query_norm, ((1,), (1,)))
        scores = (scores.reshape(shards, period, rows) + bias[None]).reshape(rows, rows)
        top = jnp.max(scores, axis=0, keepdims=True)
        powers = jnp.exp((scores - top) * scale)
        weights = powers * (1.0 / jnp.sum(powers, axis=0, keepdims=True))
        weight_grad = dot(value, grad, ((1,), (1,)))
        row_inner = jnp.sum(weights * weight_grad, axis=0, keepdims=True)
        score_grad = (weights * (weight_grad - row_inner)).astype(bf16)
        value_grad = dot(weights.astype(bf16), grad, ((1,), (0,)))
        key_norm_grad = dot(score_grad, query_norm, ((1,), (0,))) * scale
        query_norm_grad = dot(score_grad, key_norm, ((0,), (0,))) * scale
        query_grad, term = norm_back(query_norm_grad, query_unit, query_inverse, query_gain)
        query_term = query_term + term
        key_grad, term = norm_back(key_norm_grad, key_unit, key_inverse, key_gain)
        key_term = key_term + term
        store(0, h, query_grad)
        store(1, h, key_grad)
        store(2, h, value_grad)

    terms = jnp.concatenate([query_term, key_term], axis=0)
    parts = []
    for _ in range(3):
        part = terms.astype(bf16).astype(f32)
        parts.append(part)
        terms = terms - part
    parts.append(jnp.zeros_like(terms))
    piece = jnp.concatenate(parts, axis=0).astype(bf16)
    last = out_ref.shape[1] - 1
    out_ref[:, last] = jnp.broadcast_to(piece[None], (shards,) + piece.shape)


SMEM = pl.BlockSpec(memory_space=pltpu.SMEM)
VMEM = pl.BlockSpec(memory_space=pltpu.VMEM)
PARAMS = pltpu.CompilerParams(vmem_limit_bytes=40 * 1024 * 1024)


def on_device(queries, keys, values, out_grad, norm_gains, tile_image):
    shards = lax.axis_size("ctx")
    replicas = lax.axis_size("dp")
    place = lax.axis_index("ctx").astype(jnp.int32).reshape(1)
    token_rows, width = queries.shape[1:]
    tile_count = tile_image.shape[1]
    per_group = width // (GROUPS * HEAD_DIM)
    per_array = per_group * SLOTS
    tiled = (tile_count, PIECE_ROWS, width)

    sources = [x.reshape(tiled) for x in (queries, keys, values, out_grad)]
    packed = pl.pallas_call(
        pack_kernel,
        out_shape=jax.ShapeDtypeStruct(
            (shards, 4 * per_array, PIECE_ROWS, HEAD_DIM), jnp.bfloat16
        ),
        in_specs=[SMEM] + [VMEM] * 4,
        out_specs=VMEM,
        compiler_params=PARAMS,
        name="pack",
    )(tile_image, *sources)
    arrived = lax.all_to_all(packed, "ctx", split_axis=0, concat_axis=0, tiled=True)

    def body(*refs):
        work_kernel(per_group, *refs)

    worked = pl.pallas_call(
        body,
        out_shape=jax.ShapeDtypeStruct(
            (shards, 3 * per_array + 1, PIECE_ROWS, HEAD_DIM), jnp.bfloat16
        ),
        in_specs=[SMEM, SMEM, VMEM, VMEM],
        out_specs=VMEM,
        compiler_params=PARAMS,
        name="work",
    )(place, tile_image, norm_gains, arrived)
    returned = lax.all_to_all(worked, "ctx", split_axis=0, concat_axis=0, tiled=True)

    pieces = jnp.sum(returned[:, 3 * per_array, :6].astype(jnp.float32), axis=0)
    own_terms = jnp.sum(pieces.reshape(3, 2, HEAD_DIM), axis=0)
    all_terms = lax.all_to_all(
        jnp.broadcast_to(own_terms[None], (replicas, 2, HEAD_DIM)),
        "dp",
        split_axis=0,
        concat_axis=0,
        tiled=True,
    )
    gain_grad = jnp.sum(all_terms, axis=0)

    grads = pl.pallas_call(
        unpack_kernel,
        out_shape=[jax.ShapeDtypeStruct(tiled, jnp.bfloat16)] * 3,
        in_specs=[SMEM, VMEM],
        out_specs=[VMEM] * 3,
        compiler_params=PARAMS,
        name="unpack",
    )(tile_image, returned)
    grads = [x.reshape(1, token_rows, width) for x in grads]
    return (grads[0], grads[1], grads[2], gain_grad)


def solution(mesh):
    rows = P("dp", "ctx", None)
    in_specs = (rows, rows, rows, rows, P(), P("dp", None))
    out_specs = (rows, rows, rows, P())
    return jax.shard_map(
        on_device, mesh=mesh, in_specs=in_specs, out_specs=out_specs, check_vma=False
    )
```

```python
import math

import jax
import jax.numpy as jnp
from jax import lax
from jax.experimental import pallas as pl
from jax.experimental.pallas import tpu as pltpu
from jax.sharding import PartitionSpec as P

epsilon = 1e-06

GROUPS = 4
SLOTS = 2
PIECE_ROWS = 8
HEAD_DIM = 128
EARLY = 2


def packed_places(image_ref, tile_count):
    images = [image_ref[0, t] for t in range(tile_count)]
    one = jnp.int32(1)
    zero = jnp.int32(0)
    joined = [zero] + [
        jnp.where(images[t] == images[t - 1], one, zero) for t in range(1, tile_count)
    ]
    long_count = sum(joined[1:], zero)
    long_next = zero
    short_next = long_count * 2
    places = []
    for t in range(tile_count):
        ahead = joined[t + 1] if t + 1 < tile_count else zero
        in_long = joined[t] + ahead
        places.append(jnp.where(in_long > 0, long_next, short_next))
        long_next = long_next + in_long
        short_next = short_next + (1 - in_long)
    return places, long_count


def pack_kernel(image_hbm, *refs):
    sources, out_ref = refs[:4], refs[4]
    image_ref, held, image_sem, sems = refs[5:]
    tile_count = held.shape[1]
    heads = held.shape[3] // HEAD_DIM
    per_group = heads // GROUPS
    half = tile_count // 2
    image_copy = pltpu.make_async_copy(image_hbm, image_ref, image_sem)
    image_copy.start()
    copies = []
    for a, source in enumerate(sources):
        for part in range(2):
            tiles = pl.ds(part * half, half)
            copy = pltpu.make_async_copy(source.at[tiles], held.at[a, tiles], sems.at[a, part])
            copy.start()
            copies.append(copy)
    image_copy.wait()
    places, _ = packed_places(image_ref, tile_count)
    for a in range(len(sources)):
        for t in range(tile_count):
            if t % half == 0:
                copies[a * 2 + t // half].wait()
            pair = places[t] // SLOTS
            slot = places[t] % SLOTS
            for c in range(heads):
                out_ref[
                    pair * GROUPS + c // per_group,
                    (a * per_group + c % per_group) * SLOTS + slot,
                ] = held[a, t, :, c * HEAD_DIM : (c + 1) * HEAD_DIM]


def unpack_kernel(image_ref, early_ref, late_ref, *outs):
    outs, gain_ref = outs[:-1], outs[-1]
    tile_count = outs[0].shape[0]
    heads = outs[0].shape[2] // HEAD_DIM
    per_group = heads // GROUPS
    places, _ = packed_places(image_ref, tile_count)
    for a, out in enumerate(outs):
        for t in range(tile_count):
            pair = places[t] // SLOTS
            slot = places[t] % SLOTS
            for c in range(heads):
                h = c % per_group
                if h < EARLY:
                    held, piece = early_ref, (a * EARLY + h) * SLOTS
                else:
                    held, piece = late_ref, (a * (per_group - EARLY) + h - EARLY) * SLOTS
                out[t, :, c * HEAD_DIM : (c + 1) * HEAD_DIM] = held[
                    pair * GROUPS + c // per_group, piece + slot
                ]
    parts = jnp.sum(late_ref[:, late_ref.shape[1] - 1].astype(jnp.float32), axis=0)
    gain_ref[...] = parts[0:2] + parts[2:4] + parts[4:6]


def work_kernel(per_group, heads, place_ref, image_ref, gains_ref, blocks_ref, *refs):
    before_ref = refs[0] if len(refs) == 3 else None
    out_ref, terms_ref = refs[-2:]
    shards = blocks_ref.shape[0]
    tile_count = image_ref.shape[1]
    rows = shards * SLOTS * PIECE_ROWS
    scale = 1.0 / math.sqrt(HEAD_DIM)
    f32, bf16 = jnp.float32, jnp.bfloat16
    _, long_count = packed_places(image_ref, tile_count)
    is_long = place_ref[0] // GROUPS < long_count

    period = SLOTS * PIECE_ROWS
    key_slot = lax.broadcasted_iota(jnp.int32, (period, rows), 0) // PIECE_ROWS % SLOTS
    query_slot = lax.broadcasted_iota(jnp.int32, (period, rows), 1) // PIECE_ROWS % SLOTS
    apart = jnp.where(is_long, 0.0, -1e30).astype(f32)
    bias = jnp.where(key_slot == query_slot, jnp.zeros((), f32), apart)

    def load(a, h):
        first = (a * per_group + h) * SLOTS
        return blocks_ref[:, first : first + SLOTS].astype(f32).reshape(rows, HEAD_DIM)

    def store(a, h, value):
        first = (a * len(heads) + h - heads[0]) * SLOTS
        out_ref[:, first : first + SLOTS] = value.reshape(
            shards, SLOTS, PIECE_ROWS, HEAD_DIM
        ).astype(bf16)

    def normalize(raw, gain):
        inverse = lax.rsqrt(jnp.mean(raw * raw, axis=-1, keepdims=True) + epsilon)
        unit = raw * inverse
        return unit, inverse, (unit * gain).astype(bf16)

    def norm_back(grad_norm, unit, inverse, gain):
        grad = grad_norm.astype(bf16).astype(f32)
        direct = grad * gain
        inner = jnp.mean(direct * unit, axis=-1, keepdims=True)
        return inverse * (direct - unit * inner), jnp.sum(grad * unit, axis=0, keepdims=True)

    def dot(a, b, dims):
        return lax.dot_general(a, b, (dims, ((), ())), preferred_element_type=f32)

    query_gain = gains_ref[0:1, :]
    key_gain = gains_ref[1:2, :]
    query_term = jnp.zeros((1, HEAD_DIM), f32)
    key_term = jnp.zeros((1, HEAD_DIM), f32)
    for h in heads:
        query_unit, query_inverse, query_norm = normalize(load(0, h), query_gain)
        key_unit, key_inverse, key_norm = normalize(load(1, h), key_gain)
        value = load(2, h).astype(bf16)
        grad = load(3, h).astype(bf16)
        scores = dot(key_norm, query_norm, ((1,), (1,)))
        scores = (scores.reshape(shards, period, rows) + bias[None]).reshape(rows, rows)
        top = jnp.max(scores, axis=0, keepdims=True)
        powers = jnp.exp((scores - top) * scale)
        weights = powers * (1.0 / jnp.sum(powers, axis=0, keepdims=True))
        weight_grad = dot(value, grad, ((1,), (1,)))
        row_inner = jnp.sum(weights * weight_grad, axis=0, keepdims=True)
        score_grad = (weights * (weight_grad - row_inner)).astype(bf16)
        value_grad = dot(weights.astype(bf16), grad, ((1,), (0,)))
        key_norm_grad = dot(score_grad, query_norm, ((1,), (0,))) * scale
        query_norm_grad = dot(score_grad, key_norm, ((0,), (0,))) * scale
        query_grad, term = norm_back(query_norm_grad, query_unit, query_inverse, query_gain)
        query_term = query_term + term
        key_grad, term = norm_back(key_norm_grad, key_unit, key_inverse, key_gain)
        key_term = key_term + term
        store(0, h, query_grad)
        store(1, h, key_grad)
        store(2, h, value_grad)

    terms = jnp.concatenate([query_term, key_term], axis=0)
    if before_ref is not None:
        terms = terms + before_ref[...]
    terms_ref[...] = terms


def attach_kernel(terms_ref, blocks_ref, out_ref):
    last = blocks_ref.shape[1]
    out_ref[:, :last] = blocks_ref[...]
    terms = terms_ref[...]
    parts = []
    for _ in range(3):
        part = terms.astype(jnp.bfloat16).astype(jnp.float32)
        parts.append(part)
        terms = terms - part
    parts.append(jnp.zeros_like(terms))
    piece = jnp.concatenate(parts, axis=0).astype(jnp.bfloat16)
    out_ref[:, last] = jnp.broadcast_to(piece[None], out_ref[:, last].shape)


SMEM = pl.BlockSpec(memory_space=pltpu.SMEM)
VMEM = pl.BlockSpec(memory_space=pltpu.VMEM)
HBM = pl.BlockSpec(memory_space=pltpu.HBM)


def params(mib):
    return pltpu.CompilerParams(vmem_limit_bytes=mib * 1024 * 1024)


def exchange(blocks):
    return lax.all_to_all(blocks, "ctx", split_axis=0, concat_axis=0, tiled=True)


def on_device(queries, keys, values, out_grad, norm_gains, tile_image):
    bf16, f32 = jnp.bfloat16, jnp.float32
    shards = lax.axis_size("ctx")
    replicas = lax.axis_size("dp")
    place = lax.axis_index("ctx").astype(jnp.int32).reshape(1)
    token_rows, width = queries.shape[1:]
    tile_count = tile_image.shape[1]
    per_group = width // (GROUPS * HEAD_DIM)
    tiled = (tile_count, PIECE_ROWS, width)

    def blocks(pieces):
        return jax.ShapeDtypeStruct((shards, pieces, PIECE_ROWS, HEAD_DIM), bf16)

    sources = [x.reshape(tiled) for x in (queries, keys, values, out_grad)]
    packed = pl.pallas_call(
        pack_kernel,
        out_shape=blocks(4 * per_group * SLOTS),
        in_specs=[HBM] * 5,
        out_specs=VMEM,
        scratch_shapes=[
            pltpu.SMEM(tile_image.shape, jnp.int32),
            pltpu.VMEM((4,) + tiled, bf16),
            pltpu.SemaphoreType.DMA(()),
            pltpu.SemaphoreType.DMA((4, 2)),
        ],
        compiler_params=params(62),
        name="pack",
    )(tile_image, *sources)
    arrived = exchange(packed)

    def work(name, heads, *before):
        def body(*refs):
            work_kernel(per_group, heads, *refs)

        return pl.pallas_call(
            body,
            out_shape=[
                blocks(3 * len(heads) * SLOTS),
                jax.ShapeDtypeStruct(norm_gains.shape, f32),
            ],
            in_specs=[SMEM, SMEM, VMEM, VMEM] + [VMEM] * len(before),
            out_specs=[VMEM, VMEM],
            compiler_params=params(32),
            cost_estimate=pl.CostEstimate(
                flops=len(heads) * 10 * arrived.size // arrived.shape[1] * 512,
                bytes_accessed=arrived.size * 2,
                transcendentals=len(heads) * 512 * 512,
            ),
            name=name,
        )(place, tile_image, norm_gains, arrived, *before)

    early, early_terms = work("early", tuple(range(EARLY)))
    early_back = exchange(early)
    late, terms = work("late", tuple(range(EARLY, per_group)), early_terms)
    cores = [[2 * y, 2 * y + 1] for y in range(replicas // 2)]
    columns = [[2 * y + core for y in range(replicas // 2)] for core in range(2)]
    terms = lax.psum(terms, "dp", axis_index_groups=cores)
    terms = lax.psum(terms, "dp", axis_index_groups=columns)
    late = pl.pallas_call(
        attach_kernel,
        out_shape=blocks(late.shape[1] + 1),
        in_specs=[VMEM, VMEM],
        out_specs=VMEM,
        compiler_params=params(8),
        name="attach",
    )(terms, late)
    early_back, late = lax.optimization_barrier((early_back, late))
    late_back = exchange(late)

    *grads, gain_grad = pl.pallas_call(
        unpack_kernel,
        out_shape=[jax.ShapeDtypeStruct(tiled, bf16)] * 3
        + [jax.ShapeDtypeStruct(norm_gains.shape, f32)],
        in_specs=[SMEM, VMEM, VMEM],
        out_specs=[VMEM] * 4,
        compiler_params=params(16),
        name="unpack",
    )(tile_image, early_back, late_back)
    grads = [x.reshape(1, token_rows, width) for x in grads]
    return (grads[0], grads[1], grads[2], gain_grad)


def solution(mesh):
    rows = P("dp", "ctx", None)
    in_specs = (rows, rows, rows, rows, P(), P("dp", None))
    out_specs = (rows, rows, rows, P())
    return jax.shard_map(
        on_device, mesh=mesh, in_specs=in_specs, out_specs=out_specs, check_vma=False
    )
```

```python
import functools
import math

import jax
import jax.numpy as jnp
from jax import lax
from jax.experimental import pallas as pl
from jax.experimental.pallas import tpu as pltpu
from jax.sharding import PartitionSpec as P

epsilon = 1e-06

GROUPS = 4
SLOTS = 2
PIECE_ROWS = 8
HEAD_DIM = 128
PLANS = (((0, 1, 2),), ((0,), (1, 2)))
BACK = ((0,), (1, 2))


def packed_places(image_ref, tile_count):
    images = [image_ref[0, t] for t in range(tile_count)]
    one = jnp.int32(1)
    zero = jnp.int32(0)
    joined = [zero] + [
        jnp.where(images[t] == images[t - 1], one, zero) for t in range(1, tile_count)
    ]
    long_count = sum(joined[1:], zero)
    long_next = zero
    short_next = long_count * 2
    places = []
    for t in range(tile_count):
        ahead = joined[t + 1] if t + 1 < tile_count else zero
        in_long = joined[t] + ahead
        places.append(jnp.where(in_long > 0, long_next, short_next))
        long_next = long_next + in_long
        short_next = short_next + (1 - in_long)
    return places, long_count


def chunk_of(chunks):
    return {h: (i, chunk.index(h)) for i, chunk in enumerate(chunks) for h in chunk}


def pack_kernel(chunks, image_hbm, *refs):
    sources, outs = refs[:4], refs[4 : 4 + len(chunks)]
    image_ref, held, image_sem, sems = refs[4 + len(chunks) :]
    tile_count = held.shape[1]
    heads = held.shape[3] // HEAD_DIM
    per_group = heads // GROUPS
    half = tile_count // 2
    where = chunk_of(chunks)
    image_copy = pltpu.make_async_copy(image_hbm, image_ref, image_sem)
    image_copy.start()
    copies = []
    for a, source in enumerate(sources):
        for part in range(2):
            tiles = pl.ds(part * half, half)
            copy = pltpu.make_async_copy(source.at[tiles], held.at[a, tiles], sems.at[a, part])
            copy.start()
            copies.append(copy)
    image_copy.wait()
    places, _ = packed_places(image_ref, tile_count)
    for a in range(len(sources)):
        for t in range(tile_count):
            if t % half == 0:
                copies[a * 2 + t // half].wait()
            pair = places[t] // SLOTS
            slot = places[t] % SLOTS
            for c in range(heads):
                chunk, position = where[c % per_group]
                outs[chunk][
                    pair * GROUPS + c // per_group,
                    (a * len(chunks[chunk]) + position) * SLOTS + slot,
                ] = held[a, t, :, c * HEAD_DIM : (c + 1) * HEAD_DIM]


def unpack_kernel(image_ref, *refs):
    blocks, outs = refs[: len(BACK)], refs[len(BACK) :]
    tile_count = outs[0].shape[0]
    heads = outs[0].shape[2] // HEAD_DIM
    per_group = heads // GROUPS
    where = chunk_of(BACK)
    places, _ = packed_places(image_ref, tile_count)
    for a, out in enumerate(outs):
        for t in range(tile_count):
            pair = places[t] // SLOTS
            slot = places[t] % SLOTS
            for c in range(heads):
                chunk, position = where[c % per_group]
                out[t, :, c * HEAD_DIM : (c + 1) * HEAD_DIM] = blocks[chunk][
                    pair * GROUPS + c // per_group,
                    (a * len(BACK[chunk]) + position) * SLOTS + slot,
                ]


def work_kernel(last, heads, before, place_ref, image_ref, gains_ref, blocks_ref, *refs):
    if before:
        before_ref, before_terms_ref = refs[:2]
    outs = refs[-len(BACK) :] if last else refs[-2:-1]
    where = chunk_of(BACK if last else (heads,))
    lengths = [len(chunk) for chunk in (BACK if last else (heads,))]
    shards = blocks_ref.shape[0]
    tile_count = image_ref.shape[1]
    rows = shards * SLOTS * PIECE_ROWS
    scale = 1.0 / math.sqrt(HEAD_DIM)
    f32, bf16 = jnp.float32, jnp.bfloat16
    _, long_count = packed_places(image_ref, tile_count)
    is_long = place_ref[0] // GROUPS < long_count

    period = SLOTS * PIECE_ROWS
    key_slot = lax.broadcasted_iota(jnp.int32, (period, rows), 0) // PIECE_ROWS % SLOTS
    query_slot = lax.broadcasted_iota(jnp.int32, (period, rows), 1) // PIECE_ROWS % SLOTS
    apart = jnp.where(is_long, 0.0, -1e30).astype(f32)
    bias = jnp.where(key_slot == query_slot, jnp.zeros((), f32), apart)

    def load(a, h):
        first = (a * len(heads) + heads.index(h)) * SLOTS
        return blocks_ref[:, first : first + SLOTS].astype(f32).reshape(rows, HEAD_DIM)

    def store(a, h, value):
        chunk, position = where[h]
        first = (a * lengths[chunk] + position) * SLOTS
        outs[chunk][:, first : first + SLOTS] = value.reshape(
            shards, SLOTS, PIECE_ROWS, HEAD_DIM
        ).astype(bf16)

    def normalize(raw, gain):
        inverse = lax.rsqrt(jnp.mean(raw * raw, axis=-1, keepdims=True) + epsilon)
        unit = raw * inverse
        return unit, inverse, (unit * gain).astype(bf16)

    def norm_back(grad_norm, unit, inverse, gain):
        grad = grad_norm.astype(bf16).astype(f32)
        direct = grad * gain
        inner = jnp.mean(direct * unit, axis=-1, keepdims=True)
        return inverse * (direct - unit * inner), jnp.sum(grad * unit, axis=0, keepdims=True)

    def dot(a, b, dims):
        return lax.dot_general(a, b, (dims, ((), ())), preferred_element_type=f32)

    query_gain = gains_ref[0:1, :]
    key_gain = gains_ref[1:2, :]
    query_term = jnp.zeros((1, HEAD_DIM), f32)
    key_term = jnp.zeros((1, HEAD_DIM), f32)
    for h in heads:
        query_unit, query_inverse, query_norm = normalize(load(0, h), query_gain)
        key_unit, key_inverse, key_norm = normalize(load(1, h), key_gain)
        value = load(2, h).astype(bf16)
        grad = load(3, h).astype(bf16)
        scores = dot(key_norm, query_norm, ((1,), (1,)))
        scores = (scores.reshape(shards, period, rows) + bias[None]).reshape(rows, rows)
        top = jnp.max(scores, axis=0, keepdims=True)
        powers = jnp.exp((scores - top) * scale)
        weights = powers * (1.0 / jnp.sum(powers, axis=0, keepdims=True))
        weight_grad = dot(value, grad, ((1,), (1,)))
        row_inner = jnp.sum(weights * weight_grad, axis=0, keepdims=True)
        score_grad = (weights * (weight_grad - row_inner)).astype(bf16)
        value_grad = dot(weights.astype(bf16), grad, ((1,), (0,)))
        key_norm_grad = dot(score_grad, query_norm, ((1,), (0,))) * scale
        query_norm_grad = dot(score_grad, key_norm, ((0,), (0,))) * scale
        query_grad, term = norm_back(query_norm_grad, query_unit, query_inverse, query_gain)
        query_term = query_term + term
        key_grad, term = norm_back(key_norm_grad, key_unit, key_inverse, key_gain)
        key_term = key_term + term
        store(0, h, query_grad)
        store(1, h, key_grad)
        store(2, h, value_grad)

    terms = jnp.concatenate([query_term, key_term], axis=0)
    if not last:
        refs[-1][...] = terms
        return
    if before:
        terms = terms + before_terms_ref[...]
        for a in range(3):
            for i, h in enumerate(before):
                chunk, position = where[h]
                first = (a * lengths[chunk] + position) * SLOTS
                held = (a * len(before) + i) * SLOTS
                outs[chunk][:, first : first + SLOTS] = before_ref[:, held : held + SLOTS]
    parts = []
    for _ in range(3):
        part = terms.astype(bf16).astype(f32)
        parts.append(part)
        terms = terms - part
    parts.append(jnp.zeros_like(terms))
    piece = jnp.concatenate(parts, axis=0).astype(bf16)
    end = outs[0].shape[1] - 1
    outs[0][:, end] = jnp.broadcast_to(piece[None], (shards,) + piece.shape)


SMEM = pl.BlockSpec(memory_space=pltpu.SMEM)
VMEM = pl.BlockSpec(memory_space=pltpu.VMEM)
HBM = pl.BlockSpec(memory_space=pltpu.HBM)


def params(mib):
    return pltpu.CompilerParams(vmem_limit_bytes=mib * 1024 * 1024)


def exchange(blocks):
    return lax.all_to_all(blocks, "ctx", split_axis=0, concat_axis=0, tiled=True)


def blocks(shards, pieces):
    return jax.ShapeDtypeStruct((shards, pieces, PIECE_ROWS, HEAD_DIM), jnp.bfloat16)


def there(chunks, queries, keys, values, out_grad, norm_gains, tile_image):
    shards = lax.axis_size("ctx")
    place = lax.axis_index("ctx").astype(jnp.int32).reshape(1)
    sources = (queries, keys, values, out_grad)
    packed = pl.pallas_call(
        functools.partial(pack_kernel, chunks),
        out_shape=[blocks(shards, 4 * len(chunk) * SLOTS) for chunk in chunks],
        in_specs=[HBM] * 5,
        out_specs=[VMEM] * len(chunks),
        scratch_shapes=[
            pltpu.SMEM(tile_image.shape, jnp.int32),
            pltpu.VMEM((4,) + queries.shape, jnp.bfloat16),
            pltpu.SemaphoreType.DMA(()),
            pltpu.SemaphoreType.DMA((4, 2)),
        ],
        compiler_params=params(62),
        name="pack",
    )(tile_image, *sources)
    before, worked = (), []
    arrived = []
    for chunk in packed:
        if arrived:
            arrived[-1], chunk = lax.optimization_barrier((arrived[-1], chunk))
        arrived.append(exchange(chunk))
    for heads, chunk in zip(chunks, arrived):
        last = heads is chunks[-1]
        if last:
            out_shape = [
                blocks(shards, 3 * len(chunk) * SLOTS + (i == 0)) for i, chunk in enumerate(BACK)
            ]
        else:
            out_shape = [
                blocks(shards, 3 * len(heads) * SLOTS),
                jax.ShapeDtypeStruct(norm_gains.shape, jnp.float32),
            ]
        worked = pl.pallas_call(
            functools.partial(work_kernel, last, heads, before),
            out_shape=out_shape,
            in_specs=[SMEM, SMEM, VMEM, VMEM] + [VMEM] * len(worked),
            out_specs=[VMEM] * len(out_shape),
            compiler_params=params(32),
            cost_estimate=pl.CostEstimate(
                flops=len(heads) * 10 * 512 * 512 * HEAD_DIM,
                bytes_accessed=len(heads) * 7 * 512 * HEAD_DIM * 2,
                transcendentals=len(heads) * 512 * 512,
            ),
            name="work",
        )(place, tile_image, norm_gains, chunk, *worked)
        before = before + heads
    return worked


def on_device(queries, keys, values, out_grad, norm_gains, tile_image):
    token_rows, width = queries.shape[1:]
    tile_count = tile_image.shape[1]
    tiled = (tile_count, PIECE_ROWS, width)
    early, late = lax.cond(
        lax.axis_index("dp") % 2 == 0,
        functools.partial(there, PLANS[0]),
        functools.partial(there, PLANS[1]),
        *[x.reshape(tiled) for x in (queries, keys, values, out_grad)],
        norm_gains,
        tile_image,
    )
    early_back = exchange(early)
    early_back, late = lax.optimization_barrier((early_back, late))
    late_back = exchange(late)
    last = early_back.shape[1] - 1
    pieces = jnp.sum(early_back[:, last, :6].astype(jnp.float32), axis=0)
    own_terms = jnp.sum(pieces.reshape(3, 2, HEAD_DIM), axis=0)
    gain_grad = jnp.sum(lax.all_gather(own_terms, "dp"), axis=0)

    grads = pl.pallas_call(
        unpack_kernel,
        out_shape=[jax.ShapeDtypeStruct(tiled, jnp.bfloat16)] * 3,
        in_specs=[SMEM, VMEM, VMEM],
        out_specs=[VMEM] * 3,
        compiler_params=params(16),
        name="unpack",
    )(tile_image, early_back, late_back)
    return (*[x.reshape(1, token_rows, width) for x in grads], gain_grad)


def solution(mesh):
    rows = P("dp", "ctx", None)
    in_specs = (rows, rows, rows, rows, P(), P("dp", None))
    out_specs = (rows, rows, rows, P())
    return jax.shard_map(
        on_device, mesh=mesh, in_specs=in_specs, out_specs=out_specs, check_vma=False
    )
```

```python
import functools
import math

import jax
import jax.numpy as jnp
from jax import lax
from jax.experimental import pallas as pl
from jax.experimental.pallas import tpu as pltpu
from jax.sharding import PartitionSpec as P

epsilon = 1e-06

GROUPS = 4
PER_GROUP = 3
SLOTS = 2
PIECE_ROWS = 8
HEAD_DIM = 128

PLANS = (((0, 1, 2),), ((0,), (1, 2)))
BACK = ((2,), (0, 1))


def located(chunks, arrays):
    return {
        (a, h): (i, (a * len(chunk) + n) * SLOTS)
        for i, chunk in enumerate(chunks)
        for a in range(arrays)
        for n, h in enumerate(chunk)
    }


def packed_places(image_ref, tile_count):
    images = [image_ref[0, t] for t in range(tile_count)]
    one = jnp.int32(1)
    zero = jnp.int32(0)
    joined = [zero] + [
        jnp.where(images[t] == images[t - 1], one, zero) for t in range(1, tile_count)
    ]
    long_count = sum(joined[1:], zero)
    long_next = zero
    short_next = long_count * 2
    places = []
    for t in range(tile_count):
        ahead = joined[t + 1] if t + 1 < tile_count else zero
        in_long = joined[t] + ahead
        places.append(jnp.where(in_long > 0, long_next, short_next))
        long_next = long_next + in_long
        short_next = short_next + (1 - in_long)
    return places, long_count


def pack_kernel(chunks, image_hbm, *refs):
    sources, outs = refs[:4], refs[4 : 4 + len(chunks)]
    image_ref, held, image_sem, in_sems, out_sems, *packed = refs[4 + len(chunks) :]
    tile_count = held.shape[1]
    heads = held.shape[3] // HEAD_DIM
    half = tile_count // 2
    where = located(chunks, 4)
    image_copy = pltpu.make_async_copy(image_hbm, image_ref, image_sem)
    image_copy.start()
    arriving = []
    for a, source in enumerate(sources):
        for part in range(2):
            tiles = pl.ds(part * half, half)
            copy = pltpu.make_async_copy(source.at[tiles], held.at[a, tiles], in_sems.at[a, part])
            copy.start()
            arriving.append(copy)
    image_copy.wait()
    places, _ = packed_places(image_ref, tile_count)
    leaving = []
    for a in range(len(sources)):
        for t in range(tile_count):
            if t % half == 0:
                arriving[a * 2 + t // half].wait()
            pair = places[t] // SLOTS
            slot = places[t] % SLOTS
            for c in range(heads):
                chunk, piece = where[a, c % PER_GROUP]
                packed[chunk][pair * GROUPS + c // PER_GROUP, piece + slot] = held[
                    a, t, :, c * HEAD_DIM : (c + 1) * HEAD_DIM
                ]
        for i, chunk in enumerate(chunks):
            pieces = pl.ds(a * len(chunk) * SLOTS, len(chunk) * SLOTS)
            copy = pltpu.make_async_copy(
                packed[i].at[:, pieces], outs[i].at[:, pieces], out_sems.at[i, a]
            )
            copy.start()
            leaving.append(copy)
    for copy in leaving:
        copy.wait()


def unpack_kernel(image_ref, terms_ref, *refs):
    blocks = refs[: len(BACK)]
    *outs, gain_hbm, held, gain_ref, sems = refs[len(BACK) :]
    tile_count = held.shape[1]
    heads = held.shape[3] // HEAD_DIM
    where = located(BACK, len(outs))
    gain_ref[...] = jnp.sum(terms_ref[...], axis=0)
    leaving = [pltpu.make_async_copy(gain_ref, gain_hbm, sems.at[len(outs)])]
    leaving[0].start()
    places, _ = packed_places(image_ref, tile_count)
    for a, out in enumerate(outs):
        for t in range(tile_count):
            pair = places[t] // SLOTS
            slot = places[t] % SLOTS
            for c in range(heads):
                chunk, piece = where[a, c % PER_GROUP]
                held[a, t, :, c * HEAD_DIM : (c + 1) * HEAD_DIM] = blocks[chunk][
                    pair * GROUPS + c // PER_GROUP, piece + slot
                ]
        copy = pltpu.make_async_copy(held.at[a], out, sems.at[a])
        copy.start()
        leaving.append(copy)
    for copy in leaving:
        copy.wait()


def work_kernel(heads, before, long_ref, gains_ref, blocks_ref, *refs):
    last = heads[-1] == PER_GROUP - 1
    if before:
        before_ref, before_terms_ref = refs[:2]
        refs = refs[2:]
    if last:
        early_ref, late_hbm, late_ref, sems = refs
        goes_to = located(BACK, 3)
    else:
        early_ref, terms_ref = refs
        goes_to = located((heads,), 3)
    arrived_at = located((heads,), 4)
    shards = blocks_ref.shape[0]
    leaving = []

    def leave(source, piece):
        pieces = pl.ds(piece, SLOTS)
        copy = pltpu.make_async_copy(source, late_hbm.at[:, pieces], sems.at[piece // SLOTS])
        copy.start()
        leaving.append(copy)

    for (a, h), (_, piece) in located((before,), 3).items():
        leave(before_ref.at[:, pl.ds(piece, SLOTS)], goes_to[a, h][1])
    rows = shards * SLOTS * PIECE_ROWS
    scale = 1.0 / math.sqrt(HEAD_DIM)
    f32, bf16 = jnp.float32, jnp.bfloat16
    is_long = long_ref[0] > 0

    period = SLOTS * PIECE_ROWS
    key_slot = lax.broadcasted_iota(jnp.int32, (period, rows), 0) // PIECE_ROWS % SLOTS
    query_slot = lax.broadcasted_iota(jnp.int32, (period, rows), 1) // PIECE_ROWS % SLOTS
    apart = jnp.where(is_long, 0.0, -1e30).astype(f32)
    bias = jnp.where(key_slot == query_slot, jnp.zeros((), f32), apart)

    def load(a, h):
        piece = arrived_at[a, h][1]
        return blocks_ref[:, piece : piece + SLOTS].astype(f32).reshape(rows, HEAD_DIM)

    def store(a, h, value):
        chunk, piece = goes_to[a, h]
        held = late_ref if chunk else early_ref
        held[:, piece : piece + SLOTS] = value.reshape(
            shards, SLOTS, PIECE_ROWS, HEAD_DIM
        ).astype(bf16)
        if chunk:
            leave(late_ref.at[:, pl.ds(piece, SLOTS)], piece)

    def normalize(raw, gain):
        inverse = lax.rsqrt(jnp.mean(raw * raw, axis=-1, keepdims=True) + epsilon)
        unit = raw * inverse
        return unit, inverse, (unit * gain).astype(bf16)

    def norm_back(grad_norm, unit, inverse, gain):
        grad = grad_norm.astype(bf16).astype(f32)
        direct = grad * gain
        inner = jnp.mean(direct * unit, axis=-1, keepdims=True)
        return inverse * (direct - unit * inner), jnp.sum(grad * unit, axis=0, keepdims=True)

    def dot(a, b, dims):
        return lax.dot_general(a, b, (dims, ((), ())), preferred_element_type=f32)

    query_gain = gains_ref[0:1, :]
    key_gain = gains_ref[1:2, :]
    query_term = jnp.zeros((1, HEAD_DIM), f32)
    key_term = jnp.zeros((1, HEAD_DIM), f32)
    for h in heads:
        query_unit, query_inverse, query_norm = normalize(load(0, h), query_gain)
        key_unit, key_inverse, key_norm = normalize(load(1, h), key_gain)
        value = load(2, h).astype(bf16)
        grad = load(3, h).astype(bf16)
        scores = dot(key_norm, query_norm, ((1,), (1,)))
        scores = (scores.reshape(shards, period, rows) + bias[None]).reshape(rows, rows)
        top = jnp.max(scores, axis=0, keepdims=True)
        powers = jnp.exp2((scores - top) * (scale * math.log2(math.e)))
        weights = powers * (1.0 / jnp.sum(powers, axis=0, keepdims=True))
        weight_grad = dot(value, grad, ((1,), (1,)))
        row_inner = jnp.sum(weights * weight_grad, axis=0, keepdims=True)
        score_grad = (weights * (weight_grad - row_inner)).astype(bf16)
        value_grad = dot(weights.astype(bf16), grad, ((1,), (0,)))
        key_norm_grad = dot(score_grad, query_norm, ((1,), (0,))) * scale
        query_norm_grad = dot(score_grad, key_norm, ((0,), (0,))) * scale
        query_grad, term = norm_back(query_norm_grad, query_unit, query_inverse, query_gain)
        query_term = query_term + term
        key_grad, term = norm_back(key_norm_grad, key_unit, key_inverse, key_gain)
        key_term = key_term + term
        store(0, h, query_grad)
        store(1, h, key_grad)
        store(2, h, value_grad)

    terms = jnp.concatenate([query_term, key_term], axis=0)
    if not last:
        terms_ref[...] = terms
        return
    if before:
        terms = terms + before_terms_ref[...]
    parts = []
    for _ in range(3):
        part = terms.astype(bf16).astype(f32)
        parts.append(part)
        terms = terms - part
    parts.append(jnp.zeros_like(terms))
    piece = jnp.concatenate(parts, axis=0).astype(bf16)
    early_ref[:, early_ref.shape[1] - 1] = jnp.broadcast_to(piece[None], (shards,) + piece.shape)
    for copy in leaving:
        copy.wait()


SMEM = pl.BlockSpec(memory_space=pltpu.SMEM)
VMEM = pl.BlockSpec(memory_space=pltpu.VMEM)
HBM = pl.BlockSpec(memory_space=pltpu.HBM)


def params(mib):
    return pltpu.CompilerParams(vmem_limit_bytes=mib * 1024 * 1024)


def exchange(blocks):
    return lax.all_to_all(blocks, "ctx", split_axis=0, concat_axis=0, tiled=True)


def block_shape(shards, pairs, extra=0):
    return (shards, pairs * SLOTS + extra, PIECE_ROWS, HEAD_DIM)


def there(chunks, queries, keys, values, out_grad, norm_gains, tile_image):
    bf16, f32 = jnp.bfloat16, jnp.float32
    shards = lax.axis_size("ctx")
    place = lax.axis_index("ctx").astype(jnp.int32).reshape(1)
    shapes = [block_shape(shards, 4 * len(chunk)) for chunk in chunks]
    packed = pl.pallas_call(
        functools.partial(pack_kernel, chunks),
        out_shape=[jax.ShapeDtypeStruct(shape, bf16) for shape in shapes],
        in_specs=[HBM] * 5,
        out_specs=[HBM] * len(chunks),
        scratch_shapes=[
            pltpu.SMEM(tile_image.shape, jnp.int32),
            pltpu.VMEM((4,) + queries.shape, bf16),
            pltpu.SemaphoreType.DMA(()),
            pltpu.SemaphoreType.DMA((4, 2)),
            pltpu.SemaphoreType.DMA((len(chunks), 4)),
        ]
        + [pltpu.VMEM(shape, bf16) for shape in shapes],
        compiler_params=params(62),
        name="pack",
    )(tile_image, queries, keys, values, out_grad)
    *packed, tile_image = lax.optimization_barrier((*packed, tile_image))
    long_count = jnp.sum((tile_image[0, 1:] == tile_image[0, :-1]).astype(jnp.int32))
    is_long = (place // GROUPS < long_count).astype(jnp.int32)

    arrived = []
    for chunk in packed:
        if arrived:
            arrived[-1], chunk = lax.optimization_barrier((arrived[-1], chunk))
        arrived.append(exchange(chunk))

    before, worked = (), ()
    for heads, chunk in zip(chunks, arrived):
        if heads is chunks[-1]:
            early_shape, late_shape = (
                block_shape(shards, 3 * len(back), int(i == 0)) for i, back in enumerate(BACK)
            )
            out_shape = [
                jax.ShapeDtypeStruct(early_shape, bf16),
                jax.ShapeDtypeStruct(late_shape, bf16),
            ]
            out_specs = [VMEM, HBM]
            scratch_shapes = [
                pltpu.VMEM(late_shape, bf16),
                pltpu.SemaphoreType.DMA((3 * len(BACK[1]),)),
            ]
        else:
            out_shape = [
                jax.ShapeDtypeStruct(block_shape(shards, 3 * len(heads)), bf16),
                jax.ShapeDtypeStruct(norm_gains.shape, f32),
            ]
            out_specs = [VMEM, VMEM]
            scratch_shapes = []
        worked = pl.pallas_call(
            functools.partial(work_kernel, heads, before),
            out_shape=out_shape,
            in_specs=[SMEM, VMEM, VMEM] + [VMEM] * len(worked),
            out_specs=out_specs,
            scratch_shapes=scratch_shapes,
            compiler_params=params(32),
            cost_estimate=pl.CostEstimate(
                flops=len(heads) * 10 * 512 * 512 * HEAD_DIM,
                bytes_accessed=len(heads) * 7 * 512 * HEAD_DIM * 2,
                transcendentals=len(heads) * 512 * 512,
            ),
            name="work",
        )(is_long, norm_gains, chunk, *worked)
        before = before + heads
    return worked


def on_device(queries, keys, values, out_grad, norm_gains, tile_image):
    token_rows, width = queries.shape[1:]
    tile_count = tile_image.shape[1]
    tiled = (tile_count, PIECE_ROWS, width)
    early, late = lax.cond(
        lax.axis_index("dp") % 2 == 0,
        functools.partial(there, PLANS[0]),
        functools.partial(there, PLANS[1]),
        *[x.reshape(tiled) for x in (queries, keys, values, out_grad)],
        norm_gains,
        tile_image,
    )
    early_back = exchange(early)
    early_back, late = lax.optimization_barrier((early_back, late))
    late_back = exchange(late)
    last = early_back.shape[1] - 1
    pieces = jnp.sum(early_back[:, last, :6].astype(jnp.float32), axis=0)
    own_terms = jnp.sum(pieces.reshape(3, 2, HEAD_DIM), axis=0)
    all_terms = lax.all_gather(own_terms, "dp")

    *grads, gain_grad = pl.pallas_call(
        unpack_kernel,
        out_shape=[jax.ShapeDtypeStruct(tiled, jnp.bfloat16)] * 3
        + [jax.ShapeDtypeStruct(norm_gains.shape, jnp.float32)],
        in_specs=[SMEM, VMEM, VMEM, VMEM],
        out_specs=[HBM] * 4,
        scratch_shapes=[
            pltpu.VMEM((3,) + tiled, jnp.bfloat16),
            pltpu.VMEM(norm_gains.shape, jnp.float32),
            pltpu.SemaphoreType.DMA((4,)),
        ],
        compiler_params=params(16),
        name="unpack",
    )(tile_image, all_terms, early_back, late_back)
    return (*[x.reshape(1, token_rows, width) for x in grads], gain_grad)


def solution(mesh):
    rows = P("dp", "ctx", None)
    in_specs = (rows, rows, rows, rows, P(), P("dp", None))
    out_specs = (rows, rows, rows, P())
    return jax.shard_map(
        on_device, mesh=mesh, in_specs=in_specs, out_specs=out_specs, check_vma=False
    )
```

```python
import functools
import math

import jax
import jax.numpy as jnp
from jax import lax
from jax.experimental import pallas as pl
from jax.experimental.pallas import tpu as pltpu
from jax.sharding import PartitionSpec as P

epsilon = 1e-06

GROUPS = 4
PER_GROUP = 3
SLOTS = 2
PIECE_ROWS = 8
HEAD_DIM = 128

PLANS = (((0, 1, 2),), ((0,), (1, 2)))
BACK = ((2,), (0, 1))


def located(chunks, arrays):
    return {
        (a, h): (i, (a * len(chunk) + n) * SLOTS)
        for i, chunk in enumerate(chunks)
        for a in range(arrays)
        for n, h in enumerate(chunk)
    }


def packed_places(image_ref, tile_count):
    images = [image_ref[0, t] for t in range(tile_count)]
    one = jnp.int32(1)
    zero = jnp.int32(0)
    joined = [zero] + [
        jnp.where(images[t] == images[t - 1], one, zero) for t in range(1, tile_count)
    ]
    long_count = sum(joined[1:], zero)
    long_next = zero
    short_next = long_count * 2
    places = []
    for t in range(tile_count):
        ahead = joined[t + 1] if t + 1 < tile_count else zero
        in_long = joined[t] + ahead
        places.append(jnp.where(in_long > 0, long_next, short_next))
        long_next = long_next + in_long
        short_next = short_next + (1 - in_long)
    return places, long_count


def pack_kernel(heads, image_hbm, *refs):
    *sources, out_hbm, image_ref, held, packed, image_sem, in_sems, out_sems = refs
    arrays, tile_count = held.shape[:2]
    taken = len(heads) * HEAD_DIM
    image_copy = pltpu.make_async_copy(image_hbm, image_ref, image_sem)
    image_copy.start()
    arriving = []
    for a, source in enumerate(sources):
        for g in range(GROUPS):
            columns = pl.ds((g * PER_GROUP + heads[0]) * HEAD_DIM, taken)
            copy = pltpu.make_async_copy(
                source.at[:, :, columns],
                held.at[a, :, :, pl.ds(g * taken, taken)],
                in_sems.at[a, g],
            )
            copy.start()
            arriving.append(copy)
    image_copy.wait()
    places, _ = packed_places(image_ref, tile_count)
    leaving = []
    for a in range(arrays):
        for g in range(GROUPS):
            arriving[a * GROUPS + g].wait()
            for t in range(tile_count):
                pair = places[t] // SLOTS
                slot = places[t] % SLOTS
                for n in range(len(heads)):
                    first = (g * len(heads) + n) * HEAD_DIM
                    packed[pair * GROUPS + g, (a * len(heads) + n) * SLOTS + slot] = held[
                        a, t, :, first : first + HEAD_DIM
                    ]
        pieces = pl.ds(a * len(heads) * SLOTS, len(heads) * SLOTS)
        copy = pltpu.make_async_copy(
            packed.at[:, pieces], out_hbm.at[:, pieces], out_sems.at[a]
        )
        copy.start()
        leaving.append(copy)
    for copy in leaving:
        copy.wait()


def unpack_kernel(image_ref, terms_ref, *refs):
    blocks = refs[: len(BACK)]
    *outs, gain_hbm, held, gain_ref, sems = refs[len(BACK) :]
    tile_count = held.shape[1]
    heads = held.shape[3] // HEAD_DIM
    where = located(BACK, len(outs))
    gain_ref[...] = jnp.sum(terms_ref[...], axis=0)
    leaving = [pltpu.make_async_copy(gain_ref, gain_hbm, sems.at[len(outs)])]
    leaving[0].start()
    places, _ = packed_places(image_ref, tile_count)
    for a, out in enumerate(outs):
        for t in range(tile_count):
            pair = places[t] // SLOTS
            slot = places[t] % SLOTS
            for c in range(heads):
                chunk, piece = where[a, c % PER_GROUP]
                held[a, t, :, c * HEAD_DIM : (c + 1) * HEAD_DIM] = blocks[chunk][
                    pair * GROUPS + c // PER_GROUP, piece + slot
                ]
        copy = pltpu.make_async_copy(held.at[a], out, sems.at[a])
        copy.start()
        leaving.append(copy)
    for copy in leaving:
        copy.wait()


def work_kernel(heads, before, long_ref, gains_ref, blocks_ref, *refs):
    last = heads[-1] == PER_GROUP - 1
    if before:
        before_ref, before_terms_ref = refs[:2]
        refs = refs[2:]
    if last:
        early_ref, late_hbm, late_ref, sems = refs
        goes_to = located(BACK, 3)
    else:
        early_ref, terms_ref = refs
        goes_to = located((heads,), 3)
    arrived_at = located((heads,), 4)
    shards = blocks_ref.shape[0]
    leaving = []

    def leave(source, piece):
        pieces = pl.ds(piece, SLOTS)
        copy = pltpu.make_async_copy(source, late_hbm.at[:, pieces], sems.at[piece // SLOTS])
        copy.start()
        leaving.append(copy)

    for (a, h), (_, piece) in located((before,), 3).items():
        leave(before_ref.at[:, pl.ds(piece, SLOTS)], goes_to[a, h][1])
    rows = shards * SLOTS * PIECE_ROWS
    scale = 1.0 / math.sqrt(HEAD_DIM)
    f32, bf16 = jnp.float32, jnp.bfloat16
    is_long = long_ref[0] > 0

    period = SLOTS * PIECE_ROWS
    key_slot = lax.broadcasted_iota(jnp.int32, (period, rows), 0) // PIECE_ROWS % SLOTS
    query_slot = lax.broadcasted_iota(jnp.int32, (period, rows), 1) // PIECE_ROWS % SLOTS
    apart = jnp.where(is_long, 0.0, -1e30).astype(f32)
    bias = jnp.where(key_slot == query_slot, jnp.zeros((), f32), apart)

    def load(a, h):
        piece = arrived_at[a, h][1]
        return blocks_ref[:, piece : piece + SLOTS].astype(f32).reshape(rows, HEAD_DIM)

    def store(a, h, value):
        chunk, piece = goes_to[a, h]
        held = late_ref if chunk else early_ref
        held[:, piece : piece + SLOTS] = value.reshape(
            shards, SLOTS, PIECE_ROWS, HEAD_DIM
        ).astype(bf16)
        if chunk:
            leave(late_ref.at[:, pl.ds(piece, SLOTS)], piece)

    def normalize(raw, gain):
        inverse = lax.rsqrt(jnp.mean(raw * raw, axis=-1, keepdims=True) + epsilon)
        unit = raw * inverse
        return unit, inverse, (unit * gain).astype(bf16)

    def norm_back(grad_norm, unit, inverse, gain):
        grad = grad_norm.astype(bf16).astype(f32)
        direct = grad * gain
        inner = jnp.mean(direct * unit, axis=-1, keepdims=True)
        return inverse * (direct - unit * inner), jnp.sum(grad * unit, axis=0, keepdims=True)

    def dot(a, b, dims):
        return lax.dot_general(a, b, (dims, ((), ())), preferred_element_type=f32)

    query_gain = gains_ref[0:1, :]
    key_gain = gains_ref[1:2, :]
    query_term = jnp.zeros((1, HEAD_DIM), f32)
    key_term = jnp.zeros((1, HEAD_DIM), f32)
    for h in heads:
        query_unit, query_inverse, query_norm = normalize(load(0, h), query_gain)
        key_unit, key_inverse, key_norm = normalize(load(1, h), key_gain)
        value = load(2, h).astype(bf16)
        grad = load(3, h).astype(bf16)
        scores = dot(key_norm, query_norm, ((1,), (1,)))
        scores = (scores.reshape(shards, period, rows) + bias[None]).reshape(rows, rows)
        top = jnp.max(scores, axis=0, keepdims=True)
        powers = jnp.exp2((scores - top) * (scale * math.log2(math.e)))
        weights = powers * (1.0 / jnp.sum(powers, axis=0, keepdims=True))
        weight_grad = dot(value, grad, ((1,), (1,)))
        row_inner = jnp.sum(weights * weight_grad, axis=0, keepdims=True)
        score_grad = (weights * (weight_grad - row_inner)).astype(bf16)
        value_grad = dot(weights.astype(bf16), grad, ((1,), (0,)))
        key_norm_grad = dot(score_grad, query_norm, ((1,), (0,))) * scale
        query_norm_grad = dot(score_grad, key_norm, ((0,), (0,))) * scale
        query_grad, term = norm_back(query_norm_grad, query_unit, query_inverse, query_gain)
        query_term = query_term + term
        key_grad, term = norm_back(key_norm_grad, key_unit, key_inverse, key_gain)
        key_term = key_term + term
        store(0, h, query_grad)
        store(1, h, key_grad)
        store(2, h, value_grad)

    terms = jnp.concatenate([query_term, key_term], axis=0)
    if not last:
        terms_ref[...] = terms
        return
    if before:
        terms = terms + before_terms_ref[...]
    parts = []
    for _ in range(3):
        part = terms.astype(bf16).astype(f32)
        parts.append(part)
        terms = terms - part
    parts.append(jnp.zeros_like(terms))
    piece = jnp.concatenate(parts, axis=0).astype(bf16)
    early_ref[:, early_ref.shape[1] - 1] = jnp.broadcast_to(piece[None], (shards,) + piece.shape)
    for copy in leaving:
        copy.wait()


SMEM = pl.BlockSpec(memory_space=pltpu.SMEM)
VMEM = pl.BlockSpec(memory_space=pltpu.VMEM)
HBM = pl.BlockSpec(memory_space=pltpu.HBM)


def params(mib):
    return pltpu.CompilerParams(vmem_limit_bytes=mib * 1024 * 1024)


def exchange(blocks):
    return lax.all_to_all(blocks, "ctx", split_axis=0, concat_axis=0, tiled=True)


def block_shape(shards, pairs, extra=0):
    return (shards, pairs * SLOTS + extra, PIECE_ROWS, HEAD_DIM)


def there(chunks, queries, keys, values, out_grad, norm_gains, tile_image):
    bf16, f32 = jnp.bfloat16, jnp.float32
    shards = lax.axis_size("ctx")
    place = lax.axis_index("ctx").astype(jnp.int32).reshape(1)
    sources = (queries, keys, values, out_grad)
    tile_count = queries.shape[0]
    packed = []
    for heads in chunks:
        shape = block_shape(shards, 4 * len(heads))
        taken = (4, tile_count, PIECE_ROWS, GROUPS * len(heads) * HEAD_DIM)
        packed.append(
            pl.pallas_call(
                functools.partial(pack_kernel, heads),
                out_shape=jax.ShapeDtypeStruct(shape, bf16),
                in_specs=[HBM] * 5,
                out_specs=HBM,
                scratch_shapes=[
                    pltpu.SMEM(tile_image.shape, jnp.int32),
                    pltpu.VMEM(taken, bf16),
                    pltpu.VMEM(shape, bf16),
                    pltpu.SemaphoreType.DMA(()),
                    pltpu.SemaphoreType.DMA((4, GROUPS)),
                    pltpu.SemaphoreType.DMA((4,)),
                ],
                compiler_params=params(62),
                cost_estimate=pl.CostEstimate(
                    flops=0, bytes_accessed=16 * math.prod(shape), transcendentals=0
                ),
                name="pack",
            )(tile_image, *sources)
        )
    packed[0], tile_image = lax.optimization_barrier((packed[0], tile_image))
    long_count = jnp.sum((tile_image[0, 1:] == tile_image[0, :-1]).astype(jnp.int32))
    is_long = (place // GROUPS < long_count).astype(jnp.int32)

    arrived = []
    for chunk in packed:
        if arrived:
            arrived[-1], chunk = lax.optimization_barrier((arrived[-1], chunk))
        arrived.append(exchange(chunk))

    before, worked = (), ()
    for heads, chunk in zip(chunks, arrived):
        if heads is chunks[-1]:
            early_shape, late_shape = (
                block_shape(shards, 3 * len(back), int(i == 0)) for i, back in enumerate(BACK)
            )
            out_shape = [
                jax.ShapeDtypeStruct(early_shape, bf16),
                jax.ShapeDtypeStruct(late_shape, bf16),
            ]
            out_specs = [VMEM, HBM]
            scratch_shapes = [
                pltpu.VMEM(late_shape, bf16),
                pltpu.SemaphoreType.DMA((3 * len(BACK[1]),)),
            ]
        else:
            out_shape = [
                jax.ShapeDtypeStruct(block_shape(shards, 3 * len(heads)), bf16),
                jax.ShapeDtypeStruct(norm_gains.shape, f32),
            ]
            out_specs = [VMEM, VMEM]
            scratch_shapes = []
        worked = pl.pallas_call(
            functools.partial(work_kernel, heads, before),
            out_shape=out_shape,
            in_specs=[SMEM, VMEM, VMEM] + [VMEM] * len(worked),
            out_specs=out_specs,
            scratch_shapes=scratch_shapes,
            compiler_params=params(32),
            cost_estimate=pl.CostEstimate(
                flops=len(heads) * 10 * 512 * 512 * HEAD_DIM,
                bytes_accessed=len(heads) * 7 * 512 * HEAD_DIM * 2,
                transcendentals=len(heads) * 512 * 512,
            ),
            name="work",
        )(is_long, norm_gains, chunk, *worked)
        before = before + heads
    return worked


def on_device(queries, keys, values, out_grad, norm_gains, tile_image):
    token_rows, width = queries.shape[1:]
    tile_count = tile_image.shape[1]
    tiled = (tile_count, PIECE_ROWS, width)
    early, late = lax.cond(
        lax.axis_index("dp") % 2 == 0,
        functools.partial(there, PLANS[0]),
        functools.partial(there, PLANS[1]),
        *[x.reshape(tiled) for x in (queries, keys, values, out_grad)],
        norm_gains,
        tile_image,
    )
    early_back = exchange(early)
    early_back, late = lax.optimization_barrier((early_back, late))
    late_back = exchange(late)
    last = early_back.shape[1] - 1
    pieces = jnp.sum(early_back[:, last, :6].astype(jnp.float32), axis=0)
    own_terms = jnp.sum(pieces.reshape(3, 2, HEAD_DIM), axis=0)
    all_terms = lax.all_gather(own_terms, "dp")

    *grads, gain_grad = pl.pallas_call(
        unpack_kernel,
        out_shape=[jax.ShapeDtypeStruct(tiled, jnp.bfloat16)] * 3
        + [jax.ShapeDtypeStruct(norm_gains.shape, jnp.float32)],
        in_specs=[SMEM, VMEM, VMEM, VMEM],
        out_specs=[HBM] * 4,
        scratch_shapes=[
            pltpu.VMEM((3,) + tiled, jnp.bfloat16),
            pltpu.VMEM(norm_gains.shape, jnp.float32),
            pltpu.SemaphoreType.DMA((4,)),
        ],
        compiler_params=params(16),
        name="unpack",
    )(tile_image, all_terms, early_back, late_back)
    return (*[x.reshape(1, token_rows, width) for x in grads], gain_grad)


def solution(mesh):
    rows = P("dp", "ctx", None)
    in_specs = (rows, rows, rows, rows, P(), P("dp", None))
    out_specs = (rows, rows, rows, P())
    return jax.shard_map(
        on_device, mesh=mesh, in_specs=in_specs, out_specs=out_specs, check_vma=False
    )
```

```python
import functools
import math

import jax
import jax.numpy as jnp
from jax import lax
from jax.experimental import pallas as pl
from jax.experimental.pallas import tpu as pltpu
from jax.sharding import PartitionSpec as P

epsilon = 1e-06

GROUPS = 4
PER_GROUP = 3
SLOTS = 2
PIECE_ROWS = 8
HEAD_DIM = 128
ALONG_X = 4

PLANS = (((0, 1, 2),), ((0,), (1, 2)))
BACK = ((2,), (0, 1))


def located(chunks, arrays):
    return {
        (a, h): (i, (a * len(chunk) + n) * SLOTS)
        for i, chunk in enumerate(chunks)
        for a in range(arrays)
        for n, h in enumerate(chunk)
    }


def packed_places(image_ref, tile_count):
    images = [image_ref[0, t] for t in range(tile_count)]
    one = jnp.int32(1)
    zero = jnp.int32(0)
    joined = [zero] + [
        jnp.where(images[t] == images[t - 1], one, zero) for t in range(1, tile_count)
    ]
    long_count = sum(joined[1:], zero)
    long_next = zero
    short_next = long_count * 2
    places = []
    for t in range(tile_count):
        ahead = joined[t + 1] if t + 1 < tile_count else zero
        in_long = joined[t] + ahead
        places.append(jnp.where(in_long > 0, long_next, short_next))
        long_next = long_next + in_long
        short_next = short_next + (1 - in_long)
    return places, long_count


def pack_kernel(heads, image_hbm, *refs):
    *sources, out_hbm, image_ref, held, packed, image_sem, in_sems, out_sems = refs
    arrays, tile_count = held.shape[:2]
    taken = len(heads) * HEAD_DIM
    image_copy = pltpu.make_async_copy(image_hbm, image_ref, image_sem)
    image_copy.start()
    arriving = []
    for a, source in enumerate(sources):
        for g in range(GROUPS):
            columns = pl.ds((g * PER_GROUP + heads[0]) * HEAD_DIM, taken)
            copy = pltpu.make_async_copy(
                source.at[:, :, columns],
                held.at[a, :, :, pl.ds(g * taken, taken)],
                in_sems.at[a, g],
            )
            copy.start()
            arriving.append(copy)
    image_copy.wait()
    places, _ = packed_places(image_ref, tile_count)
    leaving = []
    for a in range(arrays):
        for g in range(GROUPS):
            arriving[a * GROUPS + g].wait()
            for t in range(tile_count):
                pair = places[t] // SLOTS
                slot = places[t] % SLOTS
                for n in range(len(heads)):
                    first = (g * len(heads) + n) * HEAD_DIM
                    packed[pair * GROUPS + g, (a * len(heads) + n) * SLOTS + slot] = held[
                        a, t, :, first : first + HEAD_DIM
                    ]
        pieces = pl.ds(a * len(heads) * SLOTS, len(heads) * SLOTS)
        copy = pltpu.make_async_copy(
            packed.at[:, pieces], out_hbm.at[:, pieces], out_sems.at[a]
        )
        copy.start()
        leaving.append(copy)
    for copy in leaving:
        copy.wait()


def unpack_kernel(image_ref, terms_ref, *refs):
    blocks = refs[: len(BACK)]
    *outs, gain_hbm, held, gain_ref, sems = refs[len(BACK) :]
    tile_count = held.shape[1]
    heads = held.shape[3] // HEAD_DIM
    where = located(BACK, len(outs))
    gain_ref[...] = jnp.sum(terms_ref[...], axis=0)
    leaving = [pltpu.make_async_copy(gain_ref, gain_hbm, sems.at[len(outs)])]
    leaving[0].start()
    places, _ = packed_places(image_ref, tile_count)
    for a, out in enumerate(outs):
        for t in range(tile_count):
            pair = places[t] // SLOTS
            slot = places[t] % SLOTS
            for c in range(heads):
                chunk, piece = where[a, c % PER_GROUP]
                held[a, t, :, c * HEAD_DIM : (c + 1) * HEAD_DIM] = blocks[chunk][
                    pair * GROUPS + c // PER_GROUP, piece + slot
                ]
        copy = pltpu.make_async_copy(held.at[a], out, sems.at[a])
        copy.start()
        leaving.append(copy)
    for copy in leaving:
        copy.wait()


def work_kernel(heads, before, long_ref, gains_ref, blocks_ref, *refs):
    last = heads[-1] == PER_GROUP - 1
    if before:
        before_ref, before_terms_ref = refs[:2]
        refs = refs[2:]
    if last:
        early_ref, late_hbm, late_ref, sems = refs
        goes_to = located(BACK, 3)
    else:
        early_ref, terms_ref = refs
        goes_to = located((heads,), 3)
    arrived_at = located((heads,), 4)
    shards = blocks_ref.shape[0]
    leaving = []

    def leave(source, piece):
        pieces = pl.ds(piece, SLOTS)
        copy = pltpu.make_async_copy(source, late_hbm.at[:, pieces], sems.at[piece // SLOTS])
        copy.start()
        leaving.append(copy)

    for (a, h), (_, piece) in located((before,), 3).items():
        leave(before_ref.at[:, pl.ds(piece, SLOTS)], goes_to[a, h][1])
    rows = shards * SLOTS * PIECE_ROWS
    scale = 1.0 / math.sqrt(HEAD_DIM)
    f32, bf16 = jnp.float32, jnp.bfloat16
    is_long = long_ref[0] > 0

    period = SLOTS * PIECE_ROWS
    key_slot = lax.broadcasted_iota(jnp.int32, (period, rows), 0) // PIECE_ROWS % SLOTS
    query_slot = lax.broadcasted_iota(jnp.int32, (period, rows), 1) // PIECE_ROWS % SLOTS
    apart = jnp.where(is_long, 0.0, -1e30).astype(f32)
    bias = jnp.where(key_slot == query_slot, jnp.zeros((), f32), apart)

    def load(a, h):
        piece = arrived_at[a, h][1]
        return blocks_ref[:, piece : piece + SLOTS].astype(f32).reshape(rows, HEAD_DIM)

    def store(a, h, value):
        chunk, piece = goes_to[a, h]
        held = late_ref if chunk else early_ref
        held[:, piece : piece + SLOTS] = value.reshape(
            shards, SLOTS, PIECE_ROWS, HEAD_DIM
        ).astype(bf16)
        if chunk:
            leave(late_ref.at[:, pl.ds(piece, SLOTS)], piece)

    def normalize(raw, gain):
        inverse = lax.rsqrt(jnp.mean(raw * raw, axis=-1, keepdims=True) + epsilon)
        unit = raw * inverse
        return unit, inverse, (unit * gain).astype(bf16)

    def norm_back(grad_norm, unit, inverse, gain):
        grad = grad_norm.astype(bf16).astype(f32)
        direct = grad * gain
        inner = jnp.mean(direct * unit, axis=-1, keepdims=True)
        return inverse * (direct - unit * inner), jnp.sum(grad * unit, axis=0, keepdims=True)

    def dot(a, b, dims):
        return lax.dot_general(a, b, (dims, ((), ())), preferred_element_type=f32)

    query_gain = gains_ref[0:1, :]
    key_gain = gains_ref[1:2, :]
    query_term = jnp.zeros((1, HEAD_DIM), f32)
    key_term = jnp.zeros((1, HEAD_DIM), f32)
    for h in heads:
        query_unit, query_inverse, query_norm = normalize(load(0, h), query_gain)
        key_unit, key_inverse, key_norm = normalize(load(1, h), key_gain)
        value = load(2, h).astype(bf16)
        grad = load(3, h).astype(bf16)
        scores = dot(key_norm, query_norm, ((1,), (1,)))
        scores = (scores.reshape(shards, period, rows) + bias[None]).reshape(rows, rows)
        top = jnp.max(scores, axis=0, keepdims=True)
        powers = jnp.exp2((scores - top) * (scale * math.log2(math.e)))
        weights = powers * (1.0 / jnp.sum(powers, axis=0, keepdims=True))
        weight_grad = dot(value, grad, ((1,), (1,)))
        row_inner = jnp.sum(weights * weight_grad, axis=0, keepdims=True)
        score_grad = (weights * (weight_grad - row_inner)).astype(bf16)
        value_grad = dot(weights.astype(bf16), grad, ((1,), (0,)))
        key_norm_grad = dot(score_grad, query_norm, ((1,), (0,))) * scale
        query_norm_grad = dot(score_grad, key_norm, ((0,), (0,))) * scale
        query_grad, term = norm_back(query_norm_grad, query_unit, query_inverse, query_gain)
        query_term = query_term + term
        key_grad, term = norm_back(key_norm_grad, key_unit, key_inverse, key_gain)
        key_term = key_term + term
        store(0, h, query_grad)
        store(1, h, key_grad)
        store(2, h, value_grad)

    terms = jnp.concatenate([query_term, key_term], axis=0)
    if not last:
        terms_ref[...] = terms
        return
    if before:
        terms = terms + before_terms_ref[...]
    parts = []
    for _ in range(3):
        part = terms.astype(bf16).astype(f32)
        parts.append(part)
        terms = terms - part
    parts.append(jnp.zeros_like(terms))
    piece = jnp.concatenate(parts, axis=0).astype(bf16)
    early_ref[:, early_ref.shape[1] - 1] = jnp.broadcast_to(piece[None], (shards,) + piece.shape)
    for copy in leaving:
        copy.wait()


SMEM = pl.BlockSpec(memory_space=pltpu.SMEM)
VMEM = pl.BlockSpec(memory_space=pltpu.VMEM)
HBM = pl.BlockSpec(memory_space=pltpu.HBM)


def params(mib):
    return pltpu.CompilerParams(vmem_limit_bytes=mib * 1024 * 1024)


def exchange(blocks):
    shards = lax.axis_size("ctx")
    order = [first + z * ALONG_X for first in range(ALONG_X) for z in range(shards // ALONG_X)]
    return lax.all_to_all(
        blocks, "ctx", split_axis=0, concat_axis=0, axis_index_groups=[order], tiled=True
    )


def block_shape(shards, pairs, extra=0):
    return (shards, pairs * SLOTS + extra, PIECE_ROWS, HEAD_DIM)


def there(chunks, queries, keys, values, out_grad, norm_gains, tile_image):
    bf16, f32 = jnp.bfloat16, jnp.float32
    shards = lax.axis_size("ctx")
    own = lax.axis_index("ctx").astype(jnp.int32).reshape(1)
    place = own % ALONG_X * (shards // ALONG_X) + own // ALONG_X
    sources = (queries, keys, values, out_grad)
    tile_count = queries.shape[0]
    packed = []
    for heads in chunks:
        shape = block_shape(shards, 4 * len(heads))
        taken = (4, tile_count, PIECE_ROWS, GROUPS * len(heads) * HEAD_DIM)
        packed.append(
            pl.pallas_call(
                functools.partial(pack_kernel, heads),
                out_shape=jax.ShapeDtypeStruct(shape, bf16),
                in_specs=[HBM] * 5,
                out_specs=HBM,
                scratch_shapes=[
                    pltpu.SMEM(tile_image.shape, jnp.int32),
                    pltpu.VMEM(taken, bf16),
                    pltpu.VMEM(shape, bf16),
                    pltpu.SemaphoreType.DMA(()),
                    pltpu.SemaphoreType.DMA((4, GROUPS)),
                    pltpu.SemaphoreType.DMA((4,)),
                ],
                compiler_params=params(62),
                cost_estimate=pl.CostEstimate(
                    flops=0, bytes_accessed=16 * math.prod(shape), transcendentals=0
                ),
                name="pack",
            )(tile_image, *sources)
        )
    packed[0], tile_image = lax.optimization_barrier((packed[0], tile_image))
    long_count = jnp.sum((tile_image[0, 1:] == tile_image[0, :-1]).astype(jnp.int32))
    is_long = (place // GROUPS < long_count).astype(jnp.int32)

    arrived = []
    for chunk in packed:
        if arrived:
            arrived[-1], chunk = lax.optimization_barrier((arrived[-1], chunk))
        arrived.append(exchange(chunk))

    before, worked = (), ()
    for heads, chunk in zip(chunks, arrived):
        if heads is chunks[-1]:
            early_shape, late_shape = (
                block_shape(shards, 3 * len(back), int(i == 0)) for i, back in enumerate(BACK)
            )
            out_shape = [
                jax.ShapeDtypeStruct(early_shape, bf16),
                jax.ShapeDtypeStruct(late_shape, bf16),
            ]
            out_specs = [VMEM, HBM]
            scratch_shapes = [
                pltpu.VMEM(late_shape, bf16),
                pltpu.SemaphoreType.DMA((3 * len(BACK[1]),)),
            ]
        else:
            out_shape = [
                jax.ShapeDtypeStruct(block_shape(shards, 3 * len(heads)), bf16),
                jax.ShapeDtypeStruct(norm_gains.shape, f32),
            ]
            out_specs = [VMEM, VMEM]
            scratch_shapes = []
        worked = pl.pallas_call(
            functools.partial(work_kernel, heads, before),
            out_shape=out_shape,
            in_specs=[SMEM, VMEM, VMEM] + [VMEM] * len(worked),
            out_specs=out_specs,
            scratch_shapes=scratch_shapes,
            compiler_params=params(32),
            cost_estimate=pl.CostEstimate(
                flops=len(heads) * 10 * 512 * 512 * HEAD_DIM,
                bytes_accessed=len(heads) * 7 * 512 * HEAD_DIM * 2,
                transcendentals=len(heads) * 512 * 512,
            ),
            name="work",
        )(is_long, norm_gains, chunk, *worked)
        before = before + heads
    return worked


def on_device(queries, keys, values, out_grad, norm_gains, tile_image):
    token_rows, width = queries.shape[1:]
    tile_count = tile_image.shape[1]
    tiled = (tile_count, PIECE_ROWS, width)
    early, late = lax.cond(
        lax.axis_index("dp") % 2 == 0,
        functools.partial(there, PLANS[0]),
        functools.partial(there, PLANS[1]),
        *[x.reshape(tiled) for x in (queries, keys, values, out_grad)],
        norm_gains,
        tile_image,
    )
    early_back = exchange(early)
    early_back, late = lax.optimization_barrier((early_back, late))
    late_back = exchange(late)
    last = early_back.shape[1] - 1
    pieces = jnp.sum(early_back[:, last, :6].astype(jnp.float32), axis=0)
    own_terms = jnp.sum(pieces.reshape(3, 2, HEAD_DIM), axis=0)
    all_terms = lax.all_gather(own_terms, "dp")

    *grads, gain_grad = pl.pallas_call(
        unpack_kernel,
        out_shape=[jax.ShapeDtypeStruct(tiled, jnp.bfloat16)] * 3
        + [jax.ShapeDtypeStruct(norm_gains.shape, jnp.float32)],
        in_specs=[SMEM, VMEM, VMEM, VMEM],
        out_specs=[HBM] * 4,
        scratch_shapes=[
            pltpu.VMEM((3,) + tiled, jnp.bfloat16),
            pltpu.VMEM(norm_gains.shape, jnp.float32),
            pltpu.SemaphoreType.DMA((4,)),
        ],
        compiler_params=params(16),
        name="unpack",
    )(tile_image, all_terms, early_back, late_back)
    return (*[x.reshape(1, token_rows, width) for x in grads], gain_grad)


def solution(mesh):
    rows = P("dp", "ctx", None)
    in_specs = (rows, rows, rows, rows, P(), P("dp", None))
    out_specs = (rows, rows, rows, P())
    return jax.shard_map(
        on_device, mesh=mesh, in_specs=in_specs, out_specs=out_specs, check_vma=False
    )
```
